32 devices in a mesh: dp: 2 (over core), seq: 16 (over z, y, x).
Axes of the slice: x: 2, y: 2, z: 4, core: 2. Of those that a mesh axis runs over, the one named last changes fastest.
Arguments:
- saved_mixed: bfloat16 [2, 65536, 512], P('dp', 'seq'), may hold values from -6 to 6
- out_grad: bfloat16 [2, 65536, 512], P('dp', 'seq'), may hold values from -6 to 6
- weight_in: bfloat16 [2048, 128], P('dp'), may hold values from -0.5 to 0.5
- weight_out: bfloat16 [2048, 128], P('dp'), may hold values from -0.25 to 0.25
- outer_factor: bfloat16 [256, 256], P('dp'), may hold values from -0.375 to 0.375
- inner_factor: bfloat16 [256, 256], P('dp'), may hold values from -0.375 to 0.375
- twiddle: float32 [256, 256], P(None, 'seq'), may hold values from 0.5 to 2
Outputs:
- input_grad: bfloat16 [2, 65536, 512], P('dp', 'seq')
- weight_in_grad: float32 [2048, 128], P('dp')
- weight_out_grad: float32 [2048, 128], P('dp')
The draws below stay inside these ranges and needn't reach their ends.
All inputs are finite; a program needn't handle non-finite values.
Results may differ from the reference program's by a relative error of at most 0.0062.
Values may be sent and summed in bfloat16 or wider, within the bound.
A program may use at most 128 MiB of HBM per device.

```python
import math
import jax
import jax.numpy as jnp
from jax import lax

D = 512
FF = 2048
NB = 4
BI = 256
BJ = 256
LENGTH = 65536
SEQS = 2


def block_levels(stream_key, shape, cuts, low, high):
    gain = 1.0
    for dim, parts in cuts:
        steps = jax.random.uniform(jax.random.fold_in(jax.random.fold_in(stream_key, 6), dim), (parts,), jnp.float32, low / len(cuts), high / len(cuts))
        gain = gain * jnp.repeat(jnp.exp(steps), shape[dim] // parts).reshape((-1,) + (1,) * (len(shape) - 1 - dim))
    return gain


def noise(key, dims, scale, limit, cuts=(), held_as=jnp.bfloat16):
    drawn = jax.random.normal(key, dims, jnp.float32) * scale
    if len(cuts) > 0:
        drawn = block_levels(key, dims, cuts, -0.22, 0.18) * drawn
    return jnp.clip(drawn, min=-limit, max=limit).astype(held_as)


def setup_inputs(seed: int = 0) -> dict:
    keys = jax.random.split(jax.random.key(seed), 8)
    saved_mixed = noise(keys[0], (SEQS, LENGTH, D), 1.0, 6.0, ((0, 2), (1, 16)))
    out_grad = noise(keys[1], (SEQS, LENGTH, D), 1.0, 6.0, ((0, 2), (1, 16)))
    weight_in = noise(keys[2], (FF, D // NB), (D // NB) ** -0.5, 0.5, ((0, 2),))
    weight_out = noise(keys[3], (FF, D // NB), (FF // NB) ** -0.5, 0.25, ((0, 2),))
    outer_factor = noise(keys[4], (BI, BI), BI ** -0.5, 0.375, ((0, 2),))
    inner_factor = noise(keys[5], (BJ, BJ), BJ ** -0.5, 0.375, ((0, 2),))
    twiddle = jnp.clip(jnp.exp(math.log(2.0) - 1.3862944 * jax.random.uniform(keys[6], (BI, BJ), jnp.float32) ** block_levels(keys[6], (BI, BJ), ((1, 16),), -0.2, 0.2)), 0.5, 2.0)
    return {"saved_mixed": saved_mixed, "out_grad": out_grad, "weight_in": weight_in, "weight_out": weight_out, "outer_factor": outer_factor, "inner_factor": inner_factor, "twiddle": twiddle}


def gelu_parts(pre_act):
    coeff = math.sqrt(2.0 / math.pi)
    squared = pre_act * pre_act
    tangent = jnp.tanh(coeff * (pre_act + 0.044715 * squared * pre_act))
    activated = 0.5 * pre_act * (1.0 + tangent)
    slope = 0.5 * (1.0 + tangent) + 0.5 * pre_act * (1.0 - tangent * tangent) * coeff * (1.0 + 3.0 * 0.044715 * squared)
    return (activated, slope)

def reference(saved_mixed, out_grad, weight_in, weight_out, outer_factor, inner_factor, twiddle):
    sub_width = D // NB
    hidden_block = FF // NB
    scale_factor = 1.0 / math.sqrt(SEQS * BI * BJ)

    def one_sequence(running, inputs):
        grad_in_sum, grad_out_sum = running
        saved_rows, upstream = inputs
        input_parts = []
        output_parts = []
        delta_parts = []
        for block_id in range(NB):
            saved_block = saved_rows[:, block_id * sub_width:(block_id + 1) * sub_width]
            upstream_block = upstream[:, block_id * sub_width:(block_id + 1) * sub_width]
            w_in_block = weight_in[block_id * hidden_block:(block_id + 1) * hidden_block]
            w_out_block = weight_out[block_id * hidden_block:(block_id + 1) * hidden_block]
            pre_act = jnp.dot(saved_block, w_in_block.T, preferred_element_type=jnp.float32)
            activated, gelu_slope = gelu_parts(pre_act)
            activated = activated.astype(jnp.bfloat16)
            act_grad = jnp.dot(upstream_block, w_out_block.T, preferred_element_type=jnp.float32)
            pre_grad = (act_grad * gelu_slope).astype(jnp.bfloat16)
            output_parts.append(jnp.dot(activated.T, upstream_block, preferred_element_type=jnp.float32))
            input_parts.append(jnp.dot(pre_grad.T, saved_block, preferred_element_type=jnp.float32))
            projected = jnp.dot(pre_grad, w_in_block, preferred_element_type=jnp.float32)
            delta_parts.append((upstream_block.astype(jnp.float32) + projected).astype(jnp.bfloat16))
        mixed_grad = lax.optimization_barrier(jnp.concatenate(delta_parts, axis=1))
        position_grid = mixed_grad.reshape(BI, BJ, D).astype(jnp.float32)
        outer_rows = jnp.einsum('pq,pjc->qjc', outer_factor.astype(jnp.float32), position_grid)
        turned = lax.optimization_barrier((outer_rows * twiddle[:, :, None]).astype(jnp.bfloat16))
        back_term = jnp.einsum('qpc,pj->qjc', turned.astype(jnp.float32), inner_factor.astype(jnp.float32))
        back_term = lax.optimization_barrier(back_term.astype(jnp.bfloat16))
        result = (position_grid + back_term.astype(jnp.float32)).astype(jnp.bfloat16).reshape(BI * BJ, D)
        updated = (grad_in_sum + jnp.concatenate(input_parts, axis=0), grad_out_sum + jnp.concatenate(output_parts, axis=0))
        return (updated, result)
    zeros_grad = jnp.zeros((FF, sub_width), jnp.float32)
    totals, input_grad = lax.scan(one_sequence, (zeros_grad, zeros_grad), (saved_mixed, out_grad))
    return (input_grad, totals[0] * scale_factor, totals[1] * scale_factor)
```

```python
import math

import jax
import jax.numpy as jnp
from jax import lax
from jax.sharding import PartitionSpec as P

NB = 4


def gelu_parts(pre_act):
    coeff = math.sqrt(2.0 / math.pi)
    squared = pre_act * pre_act
    tangent = jnp.tanh(coeff * (pre_act + 0.044715 * squared * pre_act))
    activated = 0.5 * pre_act * (1.0 + tangent)
    slope = 0.5 * (1.0 + tangent) + 0.5 * pre_act * (1.0 - tangent * tangent) * coeff * (
        1.0 + 3.0 * 0.044715 * squared
    )
    return (activated, slope)


def token_product(left_rows, right_rows):
    return lax.dot_general(
        left_rows, right_rows, (((0,), (0,)), ((), ())), preferred_element_type=jnp.float32
    )


def width_product(left_rows, right_rows):
    return lax.dot_general(
        left_rows, right_rows, (((1,), (1,)), ((), ())), preferred_element_type=jnp.float32
    )


def shards(saved_mixed, out_grad, weight_in, weight_out, outer_factor, inner_factor, twiddle):
    data_devices = lax.axis_size("dp")
    seq_devices = lax.axis_size("seq")
    weight_in, weight_out, outer_factor, inner_factor = (
        lax.all_gather(weight_in, "dp", axis=0, tiled=True),
        lax.all_gather(weight_out, "dp", axis=0, tiled=True),
        lax.all_gather(outer_factor, "dp", axis=0, tiled=True),
        lax.all_gather(inner_factor, "dp", axis=0, tiled=True),
    )
    seq_count, row_count, features = saved_mixed.shape
    sub_width = features // NB
    hidden_block = weight_in.shape[0] // NB
    inner_size = inner_factor.shape[0]
    local_outer = row_count // inner_size
    scale_factor = 1.0 / math.sqrt(seq_count * data_devices * row_count * seq_devices)
    saved_tokens = saved_mixed.reshape(seq_count * row_count, features)
    upstream = out_grad.reshape(seq_count * row_count, features)
    input_parts = []
    output_parts = []
    grids = []
    arrived = []
    for block_id in range(NB):
        saved_block = saved_tokens[:, block_id * sub_width : (block_id + 1) * sub_width]
        upstream_block = upstream[:, block_id * sub_width : (block_id + 1) * sub_width]
        w_in_block = weight_in[block_id * hidden_block : (block_id + 1) * hidden_block]
        w_out_block = weight_out[block_id * hidden_block : (block_id + 1) * hidden_block]
        pre_act = width_product(saved_block, w_in_block)
        activated, gelu_slope = gelu_parts(pre_act)
        activated = activated.astype(jnp.bfloat16)
        act_grad = width_product(upstream_block, w_out_block)
        pre_grad = (act_grad * gelu_slope).astype(jnp.bfloat16)
        projected = jnp.dot(pre_grad, w_in_block, preferred_element_type=jnp.float32)
        delta = (upstream_block.astype(jnp.float32) + projected).astype(jnp.bfloat16)
        grid = delta.reshape(seq_count, local_outer, inner_size, sub_width)
        grids.append(grid)
        arrived.append(lax.all_to_all(grid, "seq", split_axis=2, concat_axis=1, tiled=True))
        output_parts.append(token_product(activated, upstream_block))
        input_parts.append(token_product(pre_grad, saved_block))
    grad_in_local = jnp.concatenate(input_parts, axis=0) * scale_factor
    grad_out_local = jnp.concatenate(output_parts, axis=0) * scale_factor
    weight_in_grad, weight_out_grad = lax.psum(
        (
            lax.psum_scatter(grad_in_local, "dp", scatter_dimension=0, tiled=True),
            lax.psum_scatter(grad_out_local, "dp", scatter_dimension=0, tiled=True),
        ),
        "seq",
    )
    home = []
    for block_id in range(NB):
        outer_rows = jnp.einsum(
            "pq,spjc->sqjc",
            outer_factor,
            arrived[block_id],
            preferred_element_type=jnp.float32,
        )
        turned = (outer_rows * twiddle[None, :, :, None]).astype(jnp.bfloat16)
        home.append(lax.all_to_all(turned, "seq", split_axis=1, concat_axis=2, tiled=True))
    results = []
    for block_id in range(NB):
        back_term = jnp.einsum(
            "sipc,pj->sijc", home[block_id], inner_factor, preferred_element_type=jnp.float32
        )
        back_term = back_term.astype(jnp.bfloat16)
        results.append(
            (grids[block_id].astype(jnp.float32) + back_term.astype(jnp.float32)).astype(
                jnp.bfloat16
            )
        )
    input_grad = jnp.concatenate(results, axis=3).reshape(seq_count, row_count, features)
    return (input_grad, weight_in_grad, weight_out_grad)


def solution(mesh):
    in_specs = (
        P("dp", "seq", None),
        P("dp", "seq", None),
        P("dp", None),
        P("dp", None),
        P("dp", None),
        P("dp", None),
        P(None, "seq"),
    )
    out_specs = (P("dp", "seq", None), P("dp", None), P("dp", None))
    return jax.shard_map(shards, mesh=mesh, in_specs=in_specs, out_specs=out_specs, check_vma=False)
```

```python
import functools
import math

import jax
import jax.numpy as jnp
from jax import lax
from jax.experimental import pallas as pl
from jax.experimental.pallas import tpu as pltpu
from jax.sharding import PartitionSpec as P

NB = 4


def dot(left, right, left_dim, right_dim):
    return lax.dot_general(
        left, right, (((left_dim,), (right_dim,)), ((), ())), preferred_element_type=jnp.float32
    )


def block_kernel(
    scale_factor, sub, saved_ref, up_ref, w_in_ref, w_out_ref, w_turn_ref, delta_ref, gin_ref, gout_ref
):
    step = pl.program_id(0)
    coeff = math.sqrt(2.0 / math.pi)

    @pl.when(step == 0)
    def _():
        gin_ref[...] = jnp.zeros_like(gin_ref)
        gout_ref[...] = jnp.zeros_like(gout_ref)

    @pl.loop(0, saved_ref.shape[0] // sub)
    def _(part):
        rows = pl.ds(pl.multiple_of(part * sub, sub), sub)
        saved = saved_ref[rows, :]
        up = up_ref[rows, :]
        pre = dot(w_in_ref[...], saved, 1, 1)
        act_grad = dot(w_out_ref[...], up, 1, 1)
        squared = pre * pre
        tangent = jnp.tanh(pre * (coeff + (coeff * 0.044715) * squared))
        half = 0.5 + 0.5 * tangent
        activated = (pre * half).astype(jnp.bfloat16)
        slope = half + (pre * (1.0 - tangent * tangent)) * (
            0.5 * coeff + (1.5 * 0.044715 * coeff) * squared
        )
        pre_grad = (act_grad * slope).astype(jnp.bfloat16)
        gout_ref[...] += dot(activated, up, 1, 0)
        gin_ref[...] += dot(pre_grad, saved, 1, 0)
        projected = dot(w_turn_ref[...], pre_grad, 1, 0)
        delta_ref[rows, :] = (up.astype(jnp.float32) + projected.T).astype(jnp.bfloat16)

    @pl.when(step == pl.num_programs(0) - 1)
    def _():
        gin_ref[...] *= scale_factor
        gout_ref[...] *= scale_factor


def block_call(block_id, scale_factor, saved, up, w_in, w_out, w_turn):
    rows, features = saved.shape
    width = features // NB
    hidden = w_in.shape[0] // NB
    tile = min(1024, rows)
    tokens = pl.BlockSpec((tile, width), lambda i: (i, block_id))
    weights = pl.BlockSpec((hidden, width), lambda i: (block_id, 0))
    total = pl.BlockSpec((hidden, width), lambda i: (0, 0))
    return pl.pallas_call(
        functools.partial(block_kernel, scale_factor, min(256, tile)),
        grid=(rows // tile,),
        in_specs=[
            tokens,
            tokens,
            weights,
            weights,
            pl.BlockSpec((width, hidden), lambda i: (0, block_id)),
        ],
        out_specs=[pl.BlockSpec((tile, width), lambda i: (i, 0)), total, total],
        out_shape=[
            jax.ShapeDtypeStruct((rows, width), jnp.bfloat16),
            jax.ShapeDtypeStruct((hidden, width), jnp.float32),
            jax.ShapeDtypeStruct((hidden, width), jnp.float32),
        ],
        compiler_params=pltpu.CompilerParams(vmem_limit_bytes=58 * 1024 * 1024),
        cost_estimate=pl.CostEstimate(
            flops=10 * rows * width * hidden,
            bytes_accessed=6 * rows * width,
            transcendentals=rows * hidden,
        ),
    )(saved, up, w_in, w_out, w_turn)


def shards(saved_mixed, out_grad, weight_in, weight_out, outer_factor, inner_factor, twiddle):
    data_devices = lax.axis_size("dp")
    seq_devices = lax.axis_size("seq")
    weight_in, weight_out, outer_factor, inner_factor = (
        lax.all_gather(weight_in, "dp", axis=0, tiled=True),
        lax.all_gather(weight_out, "dp", axis=0, tiled=True),
        lax.all_gather(outer_factor, "dp", axis=0, tiled=True),
        lax.all_gather(inner_factor, "dp", axis=0, tiled=True),
    )
    seq_count, row_count, features = saved_mixed.shape
    sub_width = features // NB
    inner_size = inner_factor.shape[0]
    local_outer = row_count // inner_size
    scale_factor = 1.0 / math.sqrt(seq_count * data_devices * row_count * seq_devices)
    saved_tokens = saved_mixed.reshape(seq_count * row_count, features)
    upstream = out_grad.reshape(seq_count * row_count, features)
    input_parts = []
    output_parts = []
    grids = []
    arrived = []
    w_turn = weight_in.T
    for block_id in range(NB):
        delta, grad_in, grad_out = block_call(
            block_id, scale_factor, saved_tokens, upstream, weight_in, weight_out, w_turn
        )
        grid = delta.reshape(seq_count, local_outer, inner_size, sub_width)
        grids.append(grid)
        arrived.append(lax.all_to_all(grid, "seq", split_axis=2, concat_axis=1, tiled=True))
        input_parts.append(grad_in)
        output_parts.append(grad_out)
    both = jnp.stack([jnp.concatenate(input_parts, axis=0), jnp.concatenate(output_parts, axis=0)])
    both = lax.psum_scatter(both, "dp", scatter_dimension=1, tiled=True)
    pieces = both.reshape(2, seq_devices, both.shape[1] // seq_devices, sub_width)
    pieces = lax.all_to_all(pieces, "seq", split_axis=1, concat_axis=1, tiled=True)
    both = lax.all_gather(jnp.sum(pieces, axis=1), "seq", axis=1, tiled=True)
    weight_in_grad, weight_out_grad = both[0], both[1]
    home = []
    for block_id in range(NB):
        outer_rows = jnp.einsum(
            "pq,spjc->sqjc",
            outer_factor,
            arrived[block_id],
            preferred_element_type=jnp.float32,
        )
        turned = (outer_rows * twiddle[None, :, :, None]).astype(jnp.bfloat16)
        home.append(lax.all_to_all(turned, "seq", split_axis=1, concat_axis=2, tiled=True))
    results = []
    for block_id in range(NB):
        back_term = jnp.einsum(
            "sipc,pj->sijc", home[block_id], inner_factor, preferred_element_type=jnp.float32
        )
        back_term = back_term.astype(jnp.bfloat16)
        results.append(
            (grids[block_id].astype(jnp.float32) + back_term.astype(jnp.float32)).astype(
                jnp.bfloat16
            )
        )
    input_grad = jnp.concatenate(results, axis=3).reshape(seq_count, row_count, features)
    return (input_grad, weight_in_grad, weight_out_grad)


def solution(mesh):
    in_specs = (
        P("dp", "seq", None),
        P("dp", "seq", None),
        P("dp", None),
        P("dp", None),
        P("dp", None),
        P("dp", None),
        P(None, "seq"),
    )
    out_specs = (P("dp", "seq", None), P("dp", None), P("dp", None))
    return jax.shard_map(shards, mesh=mesh, in_specs=in_specs, out_specs=out_specs, check_vma=False)
```

```python
import functools
import math

import jax
import jax.numpy as jnp
from jax import lax
from jax.experimental import pallas as pl
from jax.experimental.pallas import tpu as pltpu
from jax.sharding import PartitionSpec as P

NB = 4


def dot(left, right, left_dim, right_dim):
    return lax.dot_general(
        left, right, (((left_dim,), (right_dim,)), ((), ())), preferred_element_type=jnp.float32
    )


def block_kernel(
    scale_factor, sub, saved_ref, up_ref, w_in_ref, w_out_ref, w_turn_ref, delta_ref, gin_ref, gout_ref
):
    step = pl.program_id(0)
    coeff = math.sqrt(2.0 / math.pi)

    @pl.when(step == 0)
    def _():
        gin_ref[...] = jnp.zeros_like(gin_ref)
        gout_ref[...] = jnp.zeros_like(gout_ref)

    @pl.loop(0, saved_ref.shape[0] // sub)
    def _(part):
        rows = pl.ds(pl.multiple_of(part * sub, sub), sub)
        saved = saved_ref[rows, :]
        up = up_ref[rows, :]
        pre = dot(w_in_ref[...], saved, 1, 1)
        act_grad = dot(w_out_ref[...], up, 1, 1)
        squared = pre * pre
        tangent = jnp.tanh(pre * (coeff + (coeff * 0.044715) * squared))
        half = 0.5 + 0.5 * tangent
        activated = (pre * half).astype(jnp.bfloat16)
        slope = half + (pre * (1.0 - tangent * tangent)) * (
            0.5 * coeff + (1.5 * 0.044715 * coeff) * squared
        )
        pre_grad = (act_grad * slope).astype(jnp.bfloat16)
        gout_ref[...] += dot(activated, up, 1, 0)
        gin_ref[...] += dot(pre_grad, saved, 1, 0)
        projected = dot(w_turn_ref[...], pre_grad, 1, 0)
        delta_ref[rows, :] = (up.astype(jnp.float32) + projected.T).astype(jnp.bfloat16)

    @pl.when(step == pl.num_programs(0) - 1)
    def _():
        gin_ref[...] *= scale_factor
        gout_ref[...] *= scale_factor


def block_call(block_id, scale_factor, saved, up, w_in, w_out, w_turn):
    rows, features = saved.shape
    width = features // NB
    hidden = w_in.shape[0] // NB
    tile = min(1024, rows)
    tokens = pl.BlockSpec((tile, width), lambda i: (i, block_id))
    weights = pl.BlockSpec((hidden, width), lambda i: (block_id, 0))
    total = pl.BlockSpec((hidden, width), lambda i: (0, 0))
    return pl.pallas_call(
        functools.partial(block_kernel, scale_factor, min(256, tile)),
        grid=(rows // tile,),
        in_specs=[
            tokens,
            tokens,
            weights,
            weights,
            pl.BlockSpec((width, hidden), lambda i: (0, block_id)),
        ],
        out_specs=[pl.BlockSpec((tile, width), lambda i: (i, 0)), total, total],
        out_shape=[
            jax.ShapeDtypeStruct((rows, width), jnp.bfloat16),
            jax.ShapeDtypeStruct((hidden, width), jnp.float32),
            jax.ShapeDtypeStruct((hidden, width), jnp.float32),
        ],
        compiler_params=pltpu.CompilerParams(vmem_limit_bytes=58 * 1024 * 1024),
        cost_estimate=pl.CostEstimate(
            flops=10 * rows * width * hidden,
            bytes_accessed=6 * rows * width,
            transcendentals=rows * hidden,
        ),
    )(saved, up, w_in, w_out, w_turn)


def shards(saved_mixed, out_grad, weight_in, weight_out, outer_factor, inner_factor, twiddle):
    data_devices = lax.axis_size("dp")
    seq_devices = lax.axis_size("seq")
    weight_in, weight_out, outer_factor, inner_factor = (
        lax.all_gather(weight_in, "dp", axis=0, tiled=True),
        lax.all_gather(weight_out, "dp", axis=0, tiled=True),
        lax.all_gather(outer_factor, "dp", axis=0, tiled=True),
        lax.all_gather(inner_factor, "dp", axis=0, tiled=True),
    )
    seq_count, row_count, features = saved_mixed.shape
    sub_width = features // NB
    inner_size = inner_factor.shape[0]
    local_outer = row_count // inner_size
    scale_factor = 1.0 / math.sqrt(seq_count * data_devices * row_count * seq_devices)
    saved_tokens = saved_mixed.reshape(seq_count * row_count, features)
    upstream = out_grad.reshape(seq_count * row_count, features)
    input_parts = []
    output_parts = []
    grids = []
    arrived = []
    w_turn = weight_in.T
    group = 2
    for first in range(0, NB, group):
        deltas = []
        for block_id in range(first, first + group):
            delta, grad_in, grad_out = block_call(
                block_id, scale_factor, saved_tokens, upstream, weight_in, weight_out, w_turn
            )
            deltas.append(delta.reshape(seq_count, local_outer, inner_size, sub_width))
            input_parts.append(grad_in)
            output_parts.append(grad_out)
        grid = jnp.concatenate(deltas, axis=3)
        grids.append(grid)
        arrived.append(lax.all_to_all(grid, "seq", split_axis=2, concat_axis=1, tiled=True))
    both = jnp.stack([jnp.concatenate(input_parts, axis=0), jnp.concatenate(output_parts, axis=0)])
    both = lax.psum_scatter(both, "dp", scatter_dimension=1, tiled=True)
    both, arrived[0] = lax.optimization_barrier((both, arrived[0]))
    pieces = both.reshape(2, seq_devices, both.shape[1] // seq_devices, sub_width)
    pieces = lax.all_to_all(pieces, "seq", split_axis=1, concat_axis=1, tiled=True)
    both = lax.all_gather(jnp.sum(pieces, axis=1), "seq", axis=1, tiled=True)
    weight_in_grad, weight_out_grad = both[0], both[1]
    home = []
    for received in arrived:
        outer_rows = jnp.einsum(
            "pq,spjc->sqjc", outer_factor, received, preferred_element_type=jnp.float32
        )
        turned = (outer_rows * twiddle[None, :, :, None]).astype(jnp.bfloat16)
        home.append(lax.all_to_all(turned, "seq", split_axis=1, concat_axis=2, tiled=True))
    results = []
    for grid, returned in zip(grids, home):
        back_term = jnp.einsum(
            "sipc,pj->sijc", returned, inner_factor, preferred_element_type=jnp.float32
        )
        back_term = back_term.astype(jnp.bfloat16)
        results.append(
            (grid.astype(jnp.float32) + back_term.astype(jnp.float32)).astype(jnp.bfloat16)
        )
    input_grad = jnp.concatenate(results, axis=3).reshape(seq_count, row_count, features)
    return (input_grad, weight_in_grad, weight_out_grad)


def solution(mesh):
    in_specs = (
        P("dp", "seq", None),
        P("dp", "seq", None),
        P("dp", None),
        P("dp", None),
        P("dp", None),
        P("dp", None),
        P(None, "seq"),
    )
    out_specs = (P("dp", "seq", None), P("dp", None), P("dp", None))
    return jax.shard_map(shards, mesh=mesh, in_specs=in_specs, out_specs=out_specs, check_vma=False)
```
